256 devices in a mesh: ctx: 16 (over z, core), tp: 16 (over y, x).
Axes of the slice: x: 4, y: 4, z: 8, core: 2. Of those that a mesh axis runs over, the one named last changes fastest.
Arguments:
- hidden_rows: bfloat16 [8192, 8192], P('ctx', 'tp'), may hold values from -6 to 6
- w_value: bfloat16 [8192, 8192], P('ctx', 'tp'), may hold values from -0.0625 to 0.0625
- w_gate: bfloat16 [8192, 8192], P('ctx', 'tp'), may hold values from -0.0625 to 0.0625
- state_proj: bfloat16 [8192, 2, 4, 256], P('ctx'), may hold values from -1.5 to 1.5
- rates: float32 [8192, 128], P('ctx', 'tp'), may hold values from 0 to 4.5, as said below
- read_weights: float32 [6, 8192, 128], P(None, 'ctx', 'tp'), may hold values from 0.25 to 2
- prior_state: float32 [128, 64, 256], P('tp'), may hold values from -24 to 24
- skip_weight: float32 [128], P('tp'), may hold values from 0.5 to 2
- norm_gain: float32 [8192], P('tp'), may hold values from 0.25 to 1.75
Outputs:
- layer_out: bfloat16 [8192, 8192], P('ctx', 'tp')
The draws below stay inside these ranges and needn't reach their ends.
Inputs may be any that keep to these rules, and one draw needn't show every extreme that they name: Positive rates.
All inputs are finite; a program needn't handle non-finite values.
Results may differ from the reference program's by a relative error of at most 0.0085.
Values may be sent and summed in bfloat16 or wider, within the bound.
No kernel may reach another device: no remote copies, remote signals or barrier semaphores. Data moves between devices by JAX's collectives and lax.ppermute only.
A program may use at most 128 MiB of HBM per device.

```python
import math
import jax
import jax.numpy as jnp
from jax import lax

D = 8192
HEADS = 128
HEAD_DIM = 64
STATE = 256
HPG = 32
LEVELS = 6
TOK_DEV = 512
TOKENS = 8192
GROUPS = 4


def draw_rates(key, part):
    keys = jax.random.split(key, 7)
    slow_share = 0.5
    is_slow = jax.random.uniform(keys[0], (HEADS,)) < slow_share
    slow_rate = jnp.exp(jax.random.uniform(keys[1], (HEADS,), minval=math.log(0.1 / TOKENS), maxval=math.log(0.6 / TOKENS)))
    fast_rate = jnp.exp(jax.random.uniform(keys[2], (HEADS,), minval=math.log(0.0025), maxval=math.log(0.04)))
    reference_decay_speed = jnp.where(is_slow, slow_rate, fast_rate)
    segment_scaling_factor = jnp.exp(jax.random.uniform(keys[3], (TOKENS // TOK_DEV, HEADS), minval=-0.7, maxval=0.7))
    segment_scaling_factor = jnp.repeat(segment_scaling_factor, TOK_DEV, axis=0)
    stochastic_shift = jax.random.uniform(keys[4], (TOKENS, HEADS), minval=0.5, maxval=2.0)
    spots = jax.random.randint(keys[5], (3,), 0, TOKENS)
    overall_quantity = jax.random.uniform(keys[6], (3, HEADS), minval=0.22, maxval=0.5)
    agreement_tally = (jnp.arange(TOKENS)[:, None] == spots[None, :]).astype(jnp.float32)
    spike_occurrences = jnp.dot(agreement_tally, overall_quantity)
    return (reference_decay_speed[None] * segment_scaling_factor * stochastic_shift + spike_occurrences).astype(jnp.float32)


def block_levels(rng, shape, pieces, low, high):
    level, own = 1.0, jax.random.fold_in(rng, 6)
    for axis_at, parts in pieces:
        steps = jnp.exp(jax.random.uniform(jax.random.fold_in(own, axis_at), (parts,), jnp.float32, low / len(pieces), high / len(pieces)))
        level = level * jnp.repeat(steps, shape[axis_at] // parts).reshape([-1 if axis == axis_at else 1 for axis in range(len(shape))])
    return level


def normal_values(key, dims, scale, most, shards=(), held_as=jnp.bfloat16):
    level = block_levels(key, dims, shards, -0.22, 0.18) if shards else 1.0
    array = jax.random.normal(key, dims, jnp.float32) * scale * level
    return jnp.minimum(jnp.maximum(array, -most), most).astype(held_as)


def setup_inputs(seed: int = 0) -> dict:
    splits = jax.random.split(jax.random.key(seed), 10)
    return {
        "hidden_rows": normal_values(splits[0], (TOKENS, D), 1.0, 6.0, ((0, 16), (1, 16))),
        "w_value": normal_values(splits[1], (D, HEADS * HEAD_DIM), D ** -0.5, 0.0625, ((0, 16), (1, 16))),
        "w_gate": normal_values(splits[2], (D, HEADS * HEAD_DIM), D ** -0.5, 0.0625, ((0, 16), (1, 16))),
        "state_proj": normal_values(splits[3], (TOKENS, 2, GROUPS, STATE), 0.25, 1.5, ((0, 16),)),
        "rates": draw_rates(jax.random.fold_in(splits[9], 71), 0),
        "read_weights": jnp.clip(jnp.exp(math.log(2.0) - 2.0794415 * jax.random.uniform(splits[5], (LEVELS, TOKENS, HEADS), jnp.float32) ** block_levels(splits[5], (LEVELS, TOKENS, HEADS), ((1, 16), (2, 16)), -0.2, 0.2)), 0.25, 2.0),
        "prior_state": normal_values(splits[6], (HEADS, HEAD_DIM, STATE), 4.0, 24.0, ((0, 16),), jnp.float32),
        "skip_weight": jnp.clip(0.5 + 1.5 * jax.random.uniform(splits[7], (HEADS,), jnp.float32) ** block_levels(splits[7], (HEADS,), ((0, 16),), -0.2, 0.2), 0.5, 2.0),
        "norm_gain": jnp.clip(1.0 + 0.15 * jax.random.normal(splits[8], (HEADS * HEAD_DIM,), jnp.float32), 0.25, 1.75),
    }


def level_of(distance, level_count):
    level = jnp.zeros(distance.shape, jnp.int32)
    for bit_pos in range(level_count):
        level = level + (jnp.right_shift(distance, bit_pos) > 0).astype(jnp.int32)
    return level

def reference(hidden_rows, w_value, w_gate, state_proj, rates, read_weights, prior_state, skip_weight, norm_gain):
    spans = TOKENS // TOK_DEV
    values_proj = jnp.dot(hidden_rows, w_value, preferred_element_type=jnp.float32).astype(jnp.bfloat16)
    gates_proj = jnp.dot(hidden_rows, w_gate, preferred_element_type=jnp.float32).astype(jnp.bfloat16)
    writes = state_proj[:, 0].astype(jnp.float32).reshape(spans, TOK_DEV, GROUPS, STATE)
    reads = state_proj[:, 1].astype(jnp.float32).reshape(spans, TOK_DEV, GROUPS, STATE)
    scores = jnp.einsum('ctgn,csgn->gcts', reads, writes)
    level_total = LEVELS - 2
    span_ids = jnp.arange(spans, dtype=jnp.int32)
    levels = level_of(jnp.bitwise_xor(span_ids[:, None], span_ids[None, :]), level_total)
    earlier = span_ids[None, :] < span_ids[:, None]
    onehot = ((levels[:, :, None] == jnp.arange(1, level_total + 1, dtype=jnp.int32)[None, None]) & earlier[:, :, None]).astype(jnp.float32)
    causal = jnp.arange(TOK_DEV)[:, None] >= jnp.arange(TOK_DEV)[None, :]

    def one_head(head_index):
        group_index = head_index // HPG
        rate_head = lax.dynamic_index_in_dim(rates, head_index, 1, keepdims=False).reshape(spans, TOK_DEV)
        cum_rate = jnp.cumsum(rate_head, axis=1)
        values_head = lax.dynamic_slice_in_dim(values_proj, head_index * HEAD_DIM, HEAD_DIM, 1).reshape(spans, TOK_DEV, HEAD_DIM)
        gates_head = lax.dynamic_slice_in_dim(gates_proj, head_index * HEAD_DIM, HEAD_DIM, 1).reshape(spans, TOK_DEV, HEAD_DIM)
        score_head = lax.dynamic_index_in_dim(scores, group_index, 0, keepdims=False)
        write_head = lax.dynamic_index_in_dim(writes, group_index, 2, keepdims=False)
        read_head = lax.dynamic_index_in_dim(reads, group_index, 2, keepdims=False)
        rate_lag = cum_rate[:, :, None] - cum_rate[:, None, :]
        mixing = (jnp.where(causal, jnp.exp(-jnp.where(causal, rate_lag, 0.0)), 0.0) * score_head).astype(jnp.bfloat16)
        local_out = jnp.einsum('cts,csp->ctp', mixing.astype(jnp.float32), values_head.astype(jnp.float32))
        span_total = cum_rate[:, -1]
        write_weighted = (jnp.exp(-(span_total[:, None] - cum_rate))[:, :, None] * write_head).astype(jnp.bfloat16)
        end_state = jnp.einsum('ctn,ctp->cpn', write_weighted.astype(jnp.float32), values_head.astype(jnp.float32))
        before = jnp.cumsum(span_total) - span_total
        exponent = jnp.where(earlier, before[:, None] - before[None, :] - span_total[None, :], 0.0)
        weight = jnp.where(earlier, jnp.exp(-exponent), 0.0)
        coefficient = onehot * weight[:, :, None]
        carried = jnp.einsum('cjl,jpn->clpn', coefficient, end_state, precision=lax.Precision.HIGHEST)
        prior_head = lax.dynamic_index_in_dim(prior_state, head_index, 0, keepdims=False)
        prior_part = jnp.exp(-before)[:, None, None] * prior_head[None]
        states = jnp.concatenate([carried, prior_part[:, None]], axis=1)
        projected = jnp.einsum('ctn,clpn->ctlp', read_head, states, precision=lax.Precision.HIGHEST)
        weights_head = lax.dynamic_index_in_dim(read_weights, head_index, 2, keepdims=False).reshape(LEVELS, spans, TOK_DEV)
        read_scale = jnp.moveaxis(weights_head[1:], 0, 2) * jnp.exp(-cum_rate)[:, :, None]
        carried_out = jnp.einsum('ctl,ctlp->ctp', read_scale, projected, precision=lax.Precision.HIGHEST)
        skip_head = lax.dynamic_index_in_dim(skip_weight, head_index, 0, keepdims=False)
        mixed_out = weights_head[0][:, :, None] * local_out + carried_out + skip_head * values_head.astype(jnp.float32)
        filtered_result = mixed_out * jax.nn.silu(gates_head.astype(jnp.float32))
        inverse = lax.rsqrt(lax.optimization_barrier(jnp.mean(filtered_result * filtered_result, axis=2, keepdims=True)) + 1e-05)
        gain_head = lax.dynamic_slice_in_dim(norm_gain, head_index * HEAD_DIM, HEAD_DIM, 0)
        return (filtered_result * inverse * gain_head).reshape(TOKENS, HEAD_DIM).astype(jnp.bfloat16)
    per_head = lax.map(one_head, jnp.arange(HEADS, dtype=jnp.int32))
    return jnp.transpose(per_head, (1, 0, 2)).reshape(TOKENS, HEADS * HEAD_DIM)
```

```python
import jax
import jax.numpy as jnp
from jax import lax
from jax.experimental import pallas as pl
from jax.experimental.pallas import tpu as pltpu
from jax.sharding import PartitionSpec as P

HEAD_DIM = 64
STATE = 256
HPG = 32
LEVELS = 6
HIGH = lax.Precision.HIGHEST
CTX = 16
SIDE = 4
ANY = pl.BlockSpec(memory_space=pl.ANY)
VMEM = pl.BlockSpec(memory_space=pltpu.VMEM)


def along_x(a, step):
    pairs = [(i, (i // SIDE) * SIDE + (i + step) % SIDE) for i in range(SIDE * SIDE)]
    return lax.ppermute(a, "tp", pairs)


def along_y(a, step):
    pairs = [(i, (i + SIDE * step) % (SIDE * SIDE)) for i in range(SIDE * SIDE)]
    return lax.ppermute(a, "tp", pairs)


def swap_ctx(a, mask):
    return lax.ppermute(a, "ctx", [(i, i ^ mask) for i in range(CTX)])


def gather_plane(rows, first, second):
    half = rows.shape[0] // 2
    lower, upper = first(rows, 1), first(rows, -1)
    far_top, far_bottom = first(lower[:half], 1), first(upper[half:], -1)
    line = jnp.concatenate([rows, lower, upper, far_top, far_bottom], axis=0)
    line_lower, line_upper = second(line, 1), second(line, -1)
    middle = line.shape[0] // 2
    line_top = second(line_lower[:middle], 1)
    line_bottom = second(line_upper[middle:], -1)
    return line, line_lower, line_upper, line_top, line_bottom


OFFSETS = (0, -1, 1, 2)


def values_kernel(*refs):
    pieces_a, pieces_b = refs[0:5], refs[5:10]
    w_ref, rows_out, values_out = refs[10:13]
    rows, weights, total, row_sem, weight_sem, out_sem = refs[13:]
    blocks, tok, depth = rows.shape
    part = tok // 2
    tp = lax.axis_index("tp")
    y, x = tp // SIDE, tp % SIDE
    for k in range(blocks):
        pltpu.make_async_copy(
            w_ref.at[pl.ds(k * depth, depth)], weights.at[k], weight_sem.at[k]
        ).start()

    def fetch(pieces, base, x_first):
        for i, near in enumerate(OFFSETS):
            for j, far in enumerate(OFFSETS):
                dx, dy = (near, far) if x_first else (far, near)
                k = ((y + dy + SIDE) % SIDE) * SIDE + (x + dx + SIDE) % SIDE
                if j < 3:
                    source = pieces[j].at[pl.ds(i * part, part)]
                else:
                    source = pieces[3 + i // 2].at[pl.ds((i % 2) * part, part)]
                pltpu.make_async_copy(
                    source, rows.at[k, pl.ds(base, part)], row_sem.at[k]
                ).start()

    fetch(pieces_a, 0, True)
    fetch(pieces_b, part, False)
    total[...] = jnp.zeros_like(total)

    @pl.loop(0, blocks)
    def _(k):
        pltpu.make_async_copy(rows.at[k], rows.at[k], row_sem.at[k]).wait()
        pltpu.make_async_copy(weights.at[k], weights.at[k], weight_sem.at[k]).wait()
        pltpu.make_async_copy(rows.at[k], rows_out.at[k], out_sem).start()
        total[...] += jnp.dot(
            rows[k], weights[k], preferred_element_type=jnp.float32
        )

    values_out[...] = total[...].astype(values_out.dtype)
    pltpu.make_async_copy(rows, rows_out, out_sem).wait()


def project_values(pieces_a, pieces_b, w_full, tok, depth):
    blocks = w_full.shape[0] // depth
    cols = w_full.shape[1]
    return pl.pallas_call(
        values_kernel,
        out_shape=(
            jax.ShapeDtypeStruct((blocks, tok, depth), jnp.bfloat16),
            jax.ShapeDtypeStruct((tok, cols), jnp.bfloat16),
        ),
        in_specs=[ANY] * 11,
        out_specs=(ANY, VMEM),
        scratch_shapes=[
            pltpu.VMEM((blocks, tok, depth), jnp.bfloat16),
            pltpu.VMEM((blocks, depth, cols), jnp.bfloat16),
            pltpu.VMEM((tok, cols), jnp.float32),
            pltpu.SemaphoreType.DMA((blocks,)),
            pltpu.SemaphoreType.DMA((blocks,)),
            pltpu.SemaphoreType.DMA,
        ],
        compiler_params=pltpu.CompilerParams(vmem_limit_bytes=32 * 2**20),
        cost_estimate=pl.CostEstimate(
            flops=2 * tok * cols * blocks * depth,
            bytes_accessed=2 * blocks * depth * (2 * tok + cols),
            transcendentals=0,
        ),
    )(*pieces_a, *pieces_b, w_full)


def gates_kernel(rows_ref, w_ref, mixed_ref, gain_ref, out_ref, rows, weights, total, row_sem, weight_sem):
    blocks, tok, depth = rows.shape
    cols = total.shape[1]
    for k in range(blocks):
        pltpu.make_async_copy(
            w_ref.at[pl.ds(k * depth, depth)], weights.at[k], weight_sem.at[k]
        ).start()
        pltpu.make_async_copy(rows_ref.at[k], rows.at[k], row_sem.at[k]).start()
    total[...] = jnp.zeros_like(total)

    @pl.loop(0, blocks)
    def _(k):
        pltpu.make_async_copy(rows.at[k], rows.at[k], row_sem.at[k]).wait()
        pltpu.make_async_copy(weights.at[k], weights.at[k], weight_sem.at[k]).wait()
        total[...] += jnp.dot(
            rows[k], weights[k], preferred_element_type=jnp.float32
        )

    gates = total[...].astype(jnp.bfloat16).astype(jnp.float32)
    gated = mixed_ref[...] * (gates / (1.0 + jnp.exp(-gates)))
    lanes = 128
    owner = lax.broadcasted_iota(jnp.int32, (cols, lanes), 0) // HEAD_DIM
    head = lax.broadcasted_iota(jnp.int32, (cols, lanes), 1)
    pick = jnp.where(owner == head, 1.0, 0.0).astype(jnp.float32)
    square_sum = jnp.dot(gated * gated, pick, precision=HIGH, preferred_element_type=jnp.float32)
    inverse = lax.rsqrt(square_sum * (1.0 / HEAD_DIM) + 1e-05)
    spread = lax.dot_general(
        inverse, pick, (((1,), (1,)), ((), ())), precision=HIGH, preferred_element_type=jnp.float32
    )
    out_ref[...] = (gated * spread * gain_ref[...]).astype(out_ref.dtype)


def finish(rows_all, w_full, mixed, gain):
    blocks, tok, depth = rows_all.shape
    cols = w_full.shape[1]
    return pl.pallas_call(
        gates_kernel,
        out_shape=jax.ShapeDtypeStruct((tok, cols), jnp.bfloat16),
        in_specs=[ANY, ANY, VMEM, VMEM],
        out_specs=VMEM,
        scratch_shapes=[
            pltpu.VMEM((blocks, tok, depth), jnp.bfloat16),
            pltpu.VMEM((blocks, depth, cols), jnp.bfloat16),
            pltpu.VMEM((tok, cols), jnp.float32),
            pltpu.SemaphoreType.DMA((blocks,)),
            pltpu.SemaphoreType.DMA((blocks,)),
        ],
        compiler_params=pltpu.CompilerParams(vmem_limit_bytes=40 * 2**20),
        cost_estimate=pl.CostEstimate(
            flops=2 * tok * cols * blocks * depth,
            bytes_accessed=2 * blocks * depth * (tok + cols),
            transcendentals=tok * cols,
        ),
    )(rows_all, w_full, mixed, gain)


def on_device(
    hidden_rows,
    w_value,
    w_gate,
    state_proj,
    rates,
    read_weights,
    prior_state,
    skip_weight,
    norm_gain,
):
    tok, heads = rates.shape
    depth = hidden_rows.shape[1]
    half = tok // 2
    me = lax.axis_index("ctx")
    core = me % 2
    plane = me // 2

    value_weights = lax.all_gather(w_value, "ctx", axis=0, tiled=True)
    gate_weights = lax.all_gather(w_gate, "ctx", axis=0, tiled=True)
    pieces_a = gather_plane(hidden_rows[:half], along_x, along_y)
    pieces_b = gather_plane(hidden_rows[half:], along_y, along_x)

    order = jnp.arange(tok)
    causal = order[:, None] >= order[None, :]
    cum_rate = jnp.dot(causal.astype(jnp.float32), rates, precision=HIGH)
    others = cum_rate[tok - 1 :]
    for bit in range(4):
        others = jnp.concatenate([others, swap_ctx(others, 1 << bit)], axis=0)
    block = jnp.arange(CTX, dtype=jnp.int32) ^ me
    between = (block[:, None] < block[None, :]) & (block[None, :] < me)
    gap = jnp.sum(jnp.where(between[:, :, None], others[None], 0.0), axis=1)
    start_rate = jnp.sum(jnp.where((block < me)[:, None], others, 0.0), axis=0)

    def total_of(distance):
        return others[distance]

    group = lax.axis_index("tp") * heads // HPG
    write_vec = lax.dynamic_index_in_dim(state_proj[:, 0], group, 1, keepdims=False)
    read_vec = lax.dynamic_index_in_dim(state_proj[:, 1], group, 1, keepdims=False)
    scores = lax.dot_general(
        read_vec, write_vec, (((1,), (1,)), ((), ())), preferred_element_type=jnp.float32
    )

    rows_all, values = project_values(pieces_a, pieces_b, value_weights, tok, depth)
    values3 = values.reshape(tok, heads, HEAD_DIM)

    span_total = cum_rate[tok - 1]
    write_weighted = (
        jnp.exp(-(span_total[None] - cum_rate))[:, :, None]
        * write_vec[:, None, :].astype(jnp.float32)
    ).astype(jnp.bfloat16)
    ends = jnp.einsum(
        "thn,thp->hpn", write_weighted, values3, preferred_element_type=jnp.float32
    )

    mine = ends.astype(jnp.bfloat16)
    sibling = swap_ctx(mine, 1)
    my_total, sibling_total = others[0], others[1]
    first_fade = jnp.where(core == 0, 1.0, 0.0)

    def fade(rate):
        return jnp.exp(-rate)

    own_scale = jnp.where(core == 0, fade(sibling_total), 1.0)
    sibling_scale = jnp.where(core == 0, 1.0, fade(my_total))
    plane_end = own_scale[:, None, None] * ends + sibling_scale[:, None, None] * sibling.astype(jnp.float32)
    share = heads // 2
    plane_share = lax.dynamic_slice_in_dim(plane_end, core * share, share, 0)
    plane_sent = plane_share.astype(jnp.bfloat16)
    near = [swap_ctx(plane_sent, 2 * m).astype(jnp.float32) for m in (1, 2, 3)]
    plane_totals = others.reshape(CTX // 2, 2, heads).sum(axis=1)
    share_totals = lax.dynamic_slice_in_dim(plane_totals, core * share, share, 1)
    planes = jnp.arange(SIDE, dtype=jnp.int32) ^ plane
    near_all = [plane_share, *near]

    def faded_sum(among):
        result = 0.0
        for m in among:
            later = jnp.zeros((share,), jnp.float32)
            for o in among:
                later = later + jnp.where((plane ^ o) > (plane ^ m), share_totals[o], 0.0)
            result = result + fade(later)[:, None, None] * near_all[m]
        return result

    pair_sum = faded_sum((2, 3)).astype(jnp.bfloat16)
    quad_sum = faded_sum((0, 1, 2, 3)).astype(jnp.bfloat16)
    quad_other = lax.ppermute(
        quad_sum, "ctx", [(2 * z + c, 2 * (7 - z) + c) for z in range(4) for c in range(2)]
    )
    shared = jnp.stack([near[0].astype(jnp.bfloat16), pair_sum, quad_other])
    shared_other = swap_ctx(shared, 1)
    lower = jnp.where(core == 0, shared, shared_other)
    upper = jnp.where(core == 0, shared_other, shared)
    states = jnp.concatenate([sibling[None], jnp.concatenate([lower, upper], axis=1)], axis=0)

    level_fade = []
    for level in range(4):
        last = (me >> level << level) - 1
        there = (me >> level) & 1
        since = jnp.sum(
            jnp.where(((block > last) & (block < me))[:, None], others, 0.0), axis=0
        )
        level_fade.append(jnp.where(there == 1, fade(since), 0.0))
    level_fade = jnp.stack(level_fade)

    prior_read = jnp.einsum(
        "tn,hpn->thp", read_vec.astype(jnp.float32), prior_state, precision=HIGH
    )
    cum_fade = jnp.exp(-cum_rate)
    rate_lag = cum_rate.T[:, :, None] - cum_rate.T[:, None, :]
    mixing = (
        jnp.where(causal[None], jnp.exp(-jnp.where(causal[None], rate_lag, 0.0)), 0.0) * scores[None]
    ).astype(jnp.bfloat16)
    local_out = jnp.einsum("hts,shp->thp", mixing, values3, preferred_element_type=jnp.float32)
    prior_scale = read_weights[5] * (cum_fade * fade(start_rate)[None])
    early = (
        read_weights[0][:, :, None] * local_out
        + prior_scale[:, :, None] * prior_read
        + skip_weight[None, :, None] * values3.astype(jnp.float32)
    )
    level_read = jnp.einsum(
        "tn,lhpn->lthp", read_vec, states, preferred_element_type=jnp.float32
    )
    level_scale = read_weights[1:5] * (cum_fade[None] * level_fade[:, None])
    mixed = early + jnp.sum(level_scale[:, :, :, None] * level_read, axis=0)

    return finish(
        rows_all, gate_weights, mixed.reshape(tok, heads * HEAD_DIM), norm_gain[None]
    )


def solution(mesh):
    in_specs = (
        P("ctx", "tp"),
        P("ctx", "tp"),
        P("ctx", "tp"),
        P("ctx", None, None, None),
        P("ctx", "tp"),
        P(None, "ctx", "tp"),
        P("tp", None, None),
        P("tp"),
        P("tp"),
    )
    out_specs = P("ctx", "tp")
    return jax.shard_map(
        on_device, mesh=mesh, in_specs=in_specs, out_specs=out_specs, check_vma=False
    )
```

```python
import jax
import jax.numpy as jnp
from jax import lax
from jax.experimental import pallas as pl
from jax.experimental.pallas import tpu as pltpu
from jax.sharding import PartitionSpec as P

HEAD_DIM = 64
STATE = 256
HPG = 32
LEVELS = 6
HIGH = lax.Precision.HIGHEST
CTX = 16
SIDE = 4
HBM = pl.BlockSpec(memory_space=pltpu.HBM)
VMEM = pl.BlockSpec(memory_space=pltpu.VMEM)


def along_x(a, step):
    pairs = [(i, (i // SIDE) * SIDE + (i + step) % SIDE) for i in range(SIDE * SIDE)]
    return lax.ppermute(a, "tp", pairs)


def along_y(a, step):
    pairs = [(i, (i + SIDE * step) % (SIDE * SIDE)) for i in range(SIDE * SIDE)]
    return lax.ppermute(a, "tp", pairs)


def swap_ctx(a, mask):
    return lax.ppermute(a, "ctx", [(i, i ^ mask) for i in range(CTX)])


OFFSETS = (0, -1, 1, 2)


def in_hbm(*arrays):
    return [pltpu.with_memory_space_constraint(a, pltpu.HBM) for a in arrays]


def copies(moves, sem):
    started = []
    for i, (source, target) in enumerate(moves):
        copy = pltpu.make_async_copy(source, target, sem.at[i])
        copy.start()
        started.append(copy)
    for copy in started:
        copy.wait()


def stack_kernel(*refs):
    sources, targets = refs[:10], refs[10:12]
    held, in_sem, out_sem = refs[12:]
    moves = []
    for line in range(2):
        at = 0
        for source in sources[5 * line : 5 * line + 5]:
            rows = source.shape[0]
            moves.append((source, held.at[line, pl.ds(at, rows)]))
            at += rows
    copies(moves, in_sem)
    copies([(held.at[line], targets[line]) for line in range(2)], out_sem)


def stack(line_a, line_b):
    rows = sum(a.shape[0] for a in line_a)
    cols = line_a[0].shape[1]
    shape = jax.ShapeDtypeStruct((rows, cols), jnp.bfloat16)
    return pl.pallas_call(
        stack_kernel,
        out_shape=(shape, shape),
        in_specs=[HBM] * 10,
        out_specs=(HBM, HBM),
        scratch_shapes=[
            pltpu.VMEM((2, rows, cols), jnp.bfloat16),
            pltpu.SemaphoreType.DMA((10,)),
            pltpu.SemaphoreType.DMA((2,)),
        ],
    )(*in_hbm(*line_a, *line_b))


def gather_rows(rows):
    half = rows.shape[0] // 2
    top, bottom = rows[:half], rows[half:]
    near = along_x(top, 1), along_x(top, -1), along_y(bottom, 1), along_y(bottom, -1)
    cut = half // 2
    part = (near[0][:cut], near[1][cut:], near[2][:cut], near[3][cut:])
    far = along_x(part[0], 1), along_x(part[1], -1), along_y(part[2], 1), along_y(part[3], -1)
    line_a, line_b = stack((top, *near[:2], *far[:2]), (bottom, *near[2:], *far[2:]))
    next_ = along_y(line_a, 1), along_y(line_a, -1), along_x(line_b, 1), along_x(line_b, -1)
    part = (next_[0][: 2 * half], next_[1][2 * half :], next_[2][: 2 * half], next_[3][2 * half :])
    last = along_y(part[0], 1), along_y(part[1], -1), along_x(part[2], 1), along_x(part[3], -1)
    return (line_a, *next_[:2], *last[:2]), (line_b, *next_[2:], *last[2:])


def fetch_weights(w_ref, weights, sem, k, slot, depth):
    apart = w_ref.shape[0] // 16
    pltpu.make_async_copy(
        w_ref.at[pl.ds(pl.multiple_of(k * apart, 16), depth)],
        weights.at[pl.ds(slot * depth, depth)],
        sem.at[slot],
    ).start()


def sources_of_slots():
    tp = lax.axis_index("tp")
    y, x = tp // SIDE, tp % SIDE
    return [
        (i, j, ((y + dy + SIDE) % SIDE) * SIDE + (x + dx + SIDE) % SIDE)
        for j, dy in enumerate(OFFSETS)
        for i, dx in enumerate(OFFSETS)
    ]


def multiply(rows, weights, total, row_sem, weight_sem):
    deep = rows.shape[1]
    depth = deep // 16
    group = 4
    for first in range(0, 16, group):
        for s in range(first, first + group):
            columns = pl.ds(s * depth, depth)
            pltpu.make_async_copy(rows.at[:, columns], rows.at[:, columns], row_sem.at[s]).wait()
            pltpu.make_async_copy(weights.at[columns], weights.at[columns], weight_sem.at[s]).wait()
        span = pl.ds(first * depth, group * depth)
        product = jnp.dot(rows[:, span], weights[span], preferred_element_type=jnp.float32)
        if first == 0:
            total[...] = product
        else:
            total[...] += product


def project_cost(tok, cols, deep):
    return pl.CostEstimate(
        flops=2 * tok * cols * deep, bytes_accessed=2 * deep * (tok + cols), transcendentals=0
    )


def fetch_and_multiply(refs, w_ref, rows, weights, total, row_sem, weight_sem):
    pieces_a, pieces_b = refs[0:5], refs[5:10]
    tok, deep = rows.shape
    depth = deep // 16
    part = tok // 2

    def piece(pieces, near, far):
        if far < 3:
            return pieces[far].at[pl.ds(near * part, part)]
        return pieces[3 + near // 2].at[pl.ds((near % 2) * part, part)]

    for slot, (i, j, k) in enumerate(sources_of_slots()):
        columns = pl.ds(slot * depth, depth)
        pltpu.make_async_copy(
            piece(pieces_a, i, j), rows.at[pl.ds(0, part), columns], row_sem.at[slot]
        ).start()
        pltpu.make_async_copy(
            piece(pieces_b, j, i), rows.at[pl.ds(part, part), columns], row_sem.at[slot]
        ).start()
        fetch_weights(w_ref, weights, weight_sem, k, slot, depth)
    multiply(rows, weights, total, row_sem, weight_sem)


def project_scratch(tok, cols, deep):
    return [
        pltpu.VMEM((tok, deep), jnp.bfloat16),
        pltpu.VMEM((deep, cols), jnp.bfloat16),
        pltpu.VMEM((tok, cols), jnp.float32),
        pltpu.SemaphoreType.DMA((16,)),
        pltpu.SemaphoreType.DMA((16,)),
    ]


def values_kernel(*refs):
    values_out, total = refs[11], refs[14]
    fetch_and_multiply(refs[:10], refs[10], *refs[12:])
    values_out[...] = total[...].astype(values_out.dtype)


def project_values(pieces, w_full, tok, depth):
    cols = w_full.shape[1]
    deep = 16 * depth
    return pl.pallas_call(
        values_kernel,
        out_shape=jax.ShapeDtypeStruct((tok, cols), jnp.bfloat16),
        in_specs=[HBM] * 11,
        out_specs=VMEM,
        scratch_shapes=project_scratch(tok, cols, deep),
        compiler_params=pltpu.CompilerParams(vmem_limit_bytes=40 * 2**20),
        cost_estimate=project_cost(tok, cols, deep),
    )(*in_hbm(*pieces, w_full))


def gates_kernel(*refs):
    mixed_ref, gain_ref, out_ref = refs[11:14]
    total = refs[16]
    fetch_and_multiply(refs[:10], refs[10], *refs[14:])
    tok, cols = total.shape
    lanes = 128
    owner = lax.broadcasted_iota(jnp.int32, (cols, lanes), 0) // HEAD_DIM
    head = lax.broadcasted_iota(jnp.int32, (cols, lanes), 1)
    pick = jnp.where(owner == head, 1.0, 0.0).astype(jnp.bfloat16)
    gain = gain_ref[...]

    def select(a, axis):
        high = a.astype(jnp.bfloat16)
        low = (a - high.astype(jnp.float32)).astype(jnp.bfloat16)
        dims = (((1,), (axis,)), ((), ()))
        return lax.dot_general(high, pick, dims, preferred_element_type=jnp.float32) + lax.dot_general(
            low, pick, dims, preferred_element_type=jnp.float32
        )

    chunk = 64
    for first in range(0, tok, chunk):
        span = pl.ds(first, chunk)
        gates = total[span].astype(jnp.bfloat16).astype(jnp.float32)
        gated = mixed_ref[span] * (gates / (1.0 + jnp.exp(-gates)))
        inverse = lax.rsqrt(select(gated * gated, 0) * (1.0 / HEAD_DIM) + 1e-05)
        out_ref[span] = (gated * select(inverse, 1) * gain).astype(out_ref.dtype)


def finish(pieces, w_full, mixed, gain):
    deep, cols = w_full.shape
    tok = mixed.shape[0]
    return pl.pallas_call(
        gates_kernel,
        out_shape=jax.ShapeDtypeStruct((tok, cols), jnp.bfloat16),
        in_specs=[HBM] * 11 + [VMEM, VMEM],
        out_specs=VMEM,
        scratch_shapes=project_scratch(tok, cols, deep),
        compiler_params=pltpu.CompilerParams(vmem_limit_bytes=40 * 2**20),
        cost_estimate=project_cost(tok, cols, deep),
    )(*in_hbm(*pieces, w_full), mixed, gain)


def on_device(
    hidden_rows,
    w_value,
    w_gate,
    state_proj,
    rates,
    read_weights,
    prior_state,
    skip_weight,
    norm_gain,
):
    tok, heads = rates.shape
    me = lax.axis_index("ctx")
    core = me % 2
    plane = me // 2

    depth = hidden_rows.shape[1]

    rest = jnp.sum(rates, axis=0)
    terms = []
    for _ in range(3):
        terms.append(lax.reduce_precision(rest, 8, 7))
        rest = rest - terms[-1]
    tail = jnp.pad(jnp.stack(terms).astype(jnp.bfloat16), ((0, 13), (0, w_value.shape[1] - heads)))
    value_weights = lax.all_gather(
        jnp.concatenate([w_value, tail], axis=0), "ctx", axis=0, tiled=True
    )
    gate_weights = lax.all_gather(w_gate, "ctx", axis=0, tiled=True)
    pieces_a, pieces_b = gather_rows(hidden_rows)
    group = lax.axis_index("tp") * heads // HPG
    rates, prior_state, read_weights, group, line = lax.optimization_barrier(
        (rates, prior_state, read_weights, group, pieces_a[0])
    )
    pieces = (line, *pieces_a[1:], *pieces_b)

    order = jnp.arange(tok)
    causal = order[:, None] >= order[None, :]
    cum_rate = jnp.dot(causal.astype(jnp.float32), rates, precision=HIGH)
    totals = value_weights.reshape(CTX, depth + 16, -1)[:, depth : depth + 3, :heads]
    totals = jnp.sum(totals.astype(jnp.float32), axis=1)
    block = jnp.arange(CTX, dtype=jnp.int32)
    start_rate = jnp.sum(jnp.where((block < me)[:, None], totals, 0.0), axis=0)

    write_vec = lax.dynamic_index_in_dim(state_proj[:, 0], group, 1, keepdims=False)
    read_vec = lax.dynamic_index_in_dim(state_proj[:, 1], group, 1, keepdims=False)
    scores = lax.dot_general(
        read_vec, write_vec, (((1,), (1,)), ((), ())), preferred_element_type=jnp.float32
    )

    values = project_values(pieces, value_weights, tok, depth)
    values3 = values.reshape(tok, heads, HEAD_DIM)

    span_total = cum_rate[tok - 1]
    write_weighted = (
        jnp.exp(-(span_total[None] - cum_rate))[:, :, None]
        * write_vec[:, None, :].astype(jnp.float32)
    ).astype(jnp.bfloat16)
    ends = jnp.einsum(
        "thn,thp->hpn", write_weighted, values3, preferred_element_type=jnp.float32
    )

    mine = ends.astype(jnp.bfloat16)
    sibling = swap_ctx(mine, 1)
    my_total = lax.dynamic_index_in_dim(totals, me, 0, keepdims=False)
    sibling_total = lax.dynamic_index_in_dim(totals, me ^ 1, 0, keepdims=False)

    def fade(rate):
        return jnp.exp(-rate)

    own_scale = jnp.where(core == 0, fade(sibling_total), 1.0)
    sibling_scale = jnp.where(core == 0, 1.0, fade(my_total))
    plane_end = own_scale[:, None, None] * ends + sibling_scale[:, None, None] * sibling.astype(jnp.float32)
    share = heads // 2
    plane_share = lax.dynamic_slice_in_dim(plane_end, core * share, share, 0)
    plane_sent = plane_share.astype(jnp.bfloat16)
    near = [swap_ctx(plane_sent, 2 * m).astype(jnp.float32) for m in (1, 2, 3)]
    plane_totals = totals.reshape(CTX // 2, 2, heads).sum(axis=1)
    share_totals = lax.dynamic_slice_in_dim(plane_totals, core * share, share, 1)
    all_planes = jnp.arange(CTX // 2, dtype=jnp.int32)
    near_all = [plane_share, *near]

    def faded_sum(among):
        result = 0.0
        for m in among:
            here = (plane ^ among[0]) // len(among)
            after = (all_planes // len(among) == here) & (all_planes > (plane ^ m))
            later = jnp.sum(jnp.where(after[:, None], share_totals, 0.0), axis=0)
            result = result + fade(later)[:, None, None] * near_all[m]
        return result

    pair_sum = faded_sum((2, 3)).astype(jnp.bfloat16)
    quad_sum = faded_sum((0, 1, 2, 3)).astype(jnp.bfloat16)
    quad_other = lax.ppermute(
        quad_sum, "ctx", [(2 * z + c, 2 * (7 - z) + c) for z in range(4) for c in range(2)]
    )
    shared = jnp.stack([near[0].astype(jnp.bfloat16), pair_sum, quad_other])
    shared_other = swap_ctx(shared, 1)
    lower = jnp.where(core == 0, shared, shared_other)
    upper = jnp.where(core == 0, shared_other, shared)
    states = jnp.concatenate([sibling[None], jnp.concatenate([lower, upper], axis=1)], axis=0)

    level_fade = []
    for level in range(4):
        last = (me >> level << level) - 1
        there = (me >> level) & 1
        since = jnp.sum(
            jnp.where(((block > last) & (block < me))[:, None], totals, 0.0), axis=0
        )
        level_fade.append(jnp.where(there == 1, fade(since), 0.0))
    level_fade = jnp.stack(level_fade)

    prior_read = jnp.einsum(
        "tn,hpn->thp", read_vec.astype(jnp.float32), prior_state, precision=HIGH
    )
    cum_fade = jnp.exp(-cum_rate)
    rate_lag = cum_rate.T[:, :, None] - cum_rate.T[:, None, :]
    mixing = (
        jnp.where(causal[None], jnp.exp(-jnp.where(causal[None], rate_lag, 0.0)), 0.0) * scores[None]
    ).astype(jnp.bfloat16)
    local_out = jnp.einsum("hts,shp->thp", mixing, values3, preferred_element_type=jnp.float32)
    prior_scale = read_weights[5] * (cum_fade * fade(start_rate)[None])
    early = (
        read_weights[0][:, :, None] * local_out
        + prior_scale[:, :, None] * prior_read
        + skip_weight[None, :, None] * values3.astype(jnp.float32)
    )
    level_read = jnp.einsum(
        "tn,lhpn->lthp", read_vec, states, preferred_element_type=jnp.float32
    )
    level_scale = read_weights[1:5] * (cum_fade[None] * level_fade[:, None])
    mixed = early + jnp.sum(level_scale[:, :, :, None] * level_read, axis=0)

    return finish(
        pieces, gate_weights, mixed.reshape(tok, heads * HEAD_DIM), norm_gain[None]
    )


def solution(mesh):
    in_specs = (
        P("ctx", "tp"),
        P("ctx", "tp"),
        P("ctx", "tp"),
        P("ctx", None, None, None),
        P("ctx", "tp"),
        P(None, "ctx", "tp"),
        P("tp", None, None),
        P("tp"),
        P("tp"),
    )
    out_specs = P("ctx", "tp")
    return jax.shard_map(
        on_device, mesh=mesh, in_specs=in_specs, out_specs=out_specs, check_vma=False
    )
```

```python
import jax
import jax.numpy as jnp
from jax import lax
from jax.experimental import pallas as pl
from jax.experimental.pallas import tpu as pltpu
from jax.sharding import PartitionSpec as P

HEAD_DIM = 64
STATE = 256
HPG = 32
LEVELS = 6
HIGH = lax.Precision.HIGHEST
CTX = 16
SIDE = 4
HBM = pl.BlockSpec(memory_space=pltpu.HBM)
VMEM = pl.BlockSpec(memory_space=pltpu.VMEM)


def along_x(a, step):
    pairs = [(i, (i // SIDE) * SIDE + (i + step) % SIDE) for i in range(SIDE * SIDE)]
    return lax.ppermute(a, "tp", pairs)


def along_y(a, step):
    pairs = [(i, (i + SIDE * step) % (SIDE * SIDE)) for i in range(SIDE * SIDE)]
    return lax.ppermute(a, "tp", pairs)


def swap_ctx(a, mask):
    return lax.ppermute(a, "ctx", [(i, i ^ mask) for i in range(CTX)])


OFFSETS = (0, -1, 1, 2)


def in_hbm(*arrays):
    return [pltpu.with_memory_space_constraint(a, pltpu.HBM) for a in arrays]


def copies(moves, sem):
    started = []
    for i, (source, target) in enumerate(moves):
        copy = pltpu.make_async_copy(source, target, sem.at[i])
        copy.start()
        started.append(copy)
    for copy in started:
        copy.wait()


def stack_kernel(*refs):
    sources, targets = refs[:10], refs[10:12]
    held, in_sem, out_sem = refs[12:]
    moves = []
    for line in range(2):
        at = 0
        for source in sources[5 * line : 5 * line + 5]:
            rows = source.shape[0]
            moves.append((source, held.at[line, pl.ds(at, rows)]))
            at += rows
    copies(moves, in_sem)
    copies([(held.at[line], targets[line]) for line in range(2)], out_sem)


def stack(line_a, line_b):
    rows = sum(a.shape[0] for a in line_a)
    cols = line_a[0].shape[1]
    shape = jax.ShapeDtypeStruct((rows, cols), jnp.bfloat16)
    return pl.pallas_call(
        stack_kernel,
        out_shape=(shape, shape),
        in_specs=[HBM] * 10,
        out_specs=(HBM, HBM),
        scratch_shapes=[
            pltpu.VMEM((2, rows, cols), jnp.bfloat16),
            pltpu.SemaphoreType.DMA((10,)),
            pltpu.SemaphoreType.DMA((2,)),
        ],
    )(*in_hbm(*line_a, *line_b))


def gather_rows(rows):
    half = rows.shape[0] // 2
    top, bottom = rows[:half], rows[half:]
    near = along_x(top, 1), along_x(top, -1), along_y(bottom, 1), along_y(bottom, -1)
    cut = half // 2
    part = (near[0][:cut], near[1][cut:], near[2][:cut], near[3][cut:])
    far = along_x(part[0], 1), along_x(part[1], -1), along_y(part[2], 1), along_y(part[3], -1)
    line_a, line_b = stack((top, *near[:2], *far[:2]), (bottom, *near[2:], *far[2:]))
    next_ = along_y(line_a, 1), along_y(line_a, -1), along_x(line_b, 1), along_x(line_b, -1)
    part = (next_[0][: 2 * half], next_[1][2 * half :], next_[2][: 2 * half], next_[3][2 * half :])
    last = along_y(part[0], 1), along_y(part[1], -1), along_x(part[2], 1), along_x(part[3], -1)
    return (line_a, *next_[:2], *last[:2]), (line_b, *next_[2:], *last[2:])


def fetch_weights(w_ref, weights, sem, k, slot, depth):
    apart = w_ref.shape[0] // 16
    pltpu.make_async_copy(
        w_ref.at[pl.ds(pl.multiple_of(k * apart, 16), depth)],
        weights.at[pl.ds(slot * depth, depth)],
        sem.at[slot],
    ).start()


def sources_of_slots():
    tp = lax.axis_index("tp")
    y, x = tp // SIDE, tp % SIDE
    return [
        (i, j, ((y + dy + SIDE) % SIDE) * SIDE + (x + dx + SIDE) % SIDE)
        for j, dy in enumerate(OFFSETS)
        for i, dx in enumerate(OFFSETS)
    ]


def multiply(rows, weights, total, row_sem, weight_sem):
    deep = rows.shape[1]
    depth = deep // 16
    group = 4
    for first in range(0, 16, group):
        for s in range(first, first + group):
            columns = pl.ds(s * depth, depth)
            pltpu.make_async_copy(rows.at[:, columns], rows.at[:, columns], row_sem.at[s]).wait()
            pltpu.make_async_copy(weights.at[columns], weights.at[columns], weight_sem.at[s]).wait()
        span = pl.ds(first * depth, group * depth)
        product = jnp.dot(rows[:, span], weights[span], preferred_element_type=jnp.float32)
        if first == 0:
            total[...] = product
        else:
            total[...] += product


def project_cost(tok, cols, deep):
    return pl.CostEstimate(
        flops=2 * tok * cols * deep, bytes_accessed=2 * deep * (tok + cols), transcendentals=0
    )


def fetch_and_multiply(refs, w_ref, rows, weights, total, row_sem, weight_sem):
    pieces_a, pieces_b = refs[0:5], refs[5:10]
    tok, deep = rows.shape
    depth = deep // 16
    part = tok // 2

    def piece(pieces, near, far):
        if far < 3:
            return pieces[far].at[pl.ds(near * part, part)]
        return pieces[3 + near // 2].at[pl.ds((near % 2) * part, part)]

    for slot, (i, j, k) in enumerate(sources_of_slots()):
        columns = pl.ds(slot * depth, depth)
        pltpu.make_async_copy(
            piece(pieces_a, i, j), rows.at[pl.ds(0, part), columns], row_sem.at[slot]
        ).start()
        pltpu.make_async_copy(
            piece(pieces_b, j, i), rows.at[pl.ds(part, part), columns], row_sem.at[slot]
        ).start()
        fetch_weights(w_ref, weights, weight_sem, k, slot, depth)
    multiply(rows, weights, total, row_sem, weight_sem)


def project_scratch(tok, cols, deep):
    return [
        pltpu.VMEM((tok, deep), jnp.bfloat16),
        pltpu.VMEM((deep, cols), jnp.bfloat16),
        pltpu.VMEM((tok, cols), jnp.float32),
        pltpu.SemaphoreType.DMA((16,)),
        pltpu.SemaphoreType.DMA((16,)),
    ]


def values_kernel(*refs):
    values_out, total = refs[11], refs[14]
    fetch_and_multiply(refs[:10], refs[10], *refs[12:])
    values_out[...] = total[...].astype(values_out.dtype)


def project_values(pieces, w_full, tok, depth):
    cols = w_full.shape[1]
    deep = 16 * depth
    return pl.pallas_call(
        values_kernel,
        out_shape=jax.ShapeDtypeStruct((tok, cols), jnp.bfloat16),
        in_specs=[HBM] * 11,
        out_specs=VMEM,
        scratch_shapes=project_scratch(tok, cols, deep),
        compiler_params=pltpu.CompilerParams(vmem_limit_bytes=40 * 2**20),
        cost_estimate=project_cost(tok, cols, deep),
    )(*in_hbm(*pieces, w_full))


def gates_kernel(*refs):
    mixed_ref, gain_ref, out_ref = refs[11:14]
    total = refs[16]
    fetch_and_multiply(refs[:10], refs[10], *refs[14:])
    tok, cols = total.shape
    lanes = 128
    owner = lax.broadcasted_iota(jnp.int32, (cols, lanes), 0) // HEAD_DIM
    head = lax.broadcasted_iota(jnp.int32, (cols, lanes), 1)
    pick = jnp.where(owner == head, 1.0, 0.0).astype(jnp.bfloat16)
    gain = gain_ref[...]

    def select(a, axis):
        high = a.astype(jnp.bfloat16)
        low = (a - high.astype(jnp.float32)).astype(jnp.bfloat16)
        dims = (((1,), (axis,)), ((), ()))
        return lax.dot_general(high, pick, dims, preferred_element_type=jnp.float32) + lax.dot_general(
            low, pick, dims, preferred_element_type=jnp.float32
        )

    chunk = 64
    for first in range(0, tok, chunk):
        span = pl.ds(first, chunk)
        gates = total[span].astype(jnp.bfloat16).astype(jnp.float32)
        gated = mixed_ref[span] * (gates / (1.0 + jnp.exp(-gates)))
        inverse = lax.rsqrt(select(gated * gated, 0) * (1.0 / HEAD_DIM) + 1e-05)
        out_ref[span] = (gated * select(inverse, 1) * gain).astype(out_ref.dtype)


def finish(pieces, w_full, mixed, gain):
    deep, cols = w_full.shape
    tok = mixed.shape[0]
    return pl.pallas_call(
        gates_kernel,
        out_shape=jax.ShapeDtypeStruct((tok, cols), jnp.bfloat16),
        in_specs=[HBM] * 11 + [VMEM, VMEM],
        out_specs=VMEM,
        scratch_shapes=project_scratch(tok, cols, deep),
        compiler_params=pltpu.CompilerParams(vmem_limit_bytes=40 * 2**20),
        cost_estimate=project_cost(tok, cols, deep),
    )(*in_hbm(*pieces, w_full), mixed, gain)


def on_device(
    hidden_rows,
    w_value,
    w_gate,
    state_proj,
    rates,
    read_weights,
    prior_state,
    skip_weight,
    norm_gain,
):
    tok, heads = rates.shape
    me = lax.axis_index("ctx")
    core = me % 2
    plane = me // 2

    depth = hidden_rows.shape[1]

    rest = jnp.sum(rates, axis=0)
    terms = []
    for _ in range(3):
        terms.append(lax.reduce_precision(rest, 8, 7))
        rest = rest - terms[-1]
    tail = jnp.pad(jnp.stack(terms).astype(jnp.bfloat16), ((0, 13), (0, w_value.shape[1] - heads)))
    value_weights = lax.all_gather(
        jnp.concatenate([w_value, tail], axis=0), "ctx", axis=0, tiled=True
    )
    gate_weights = lax.all_gather(w_gate, "ctx", axis=0, tiled=True)
    pieces_a, pieces_b = gather_rows(hidden_rows)
    group = lax.axis_index("tp") * heads // HPG
    rates, prior_state, read_weights, group, line = lax.optimization_barrier(
        (rates, prior_state, read_weights, group, pieces_a[0])
    )
    pieces = (line, *pieces_a[1:], *pieces_b)

    order = jnp.arange(tok)
    causal = order[:, None] >= order[None, :]
    cum_rate = jnp.dot(causal.astype(jnp.float32), rates, precision=HIGH)
    totals = value_weights.reshape(CTX, depth + 16, -1)[:, depth : depth + 3, :heads]
    totals = jnp.sum(totals.astype(jnp.float32), axis=1)
    block = jnp.arange(CTX, dtype=jnp.int32)
    start_rate = jnp.sum(jnp.where((block < me)[:, None], totals, 0.0), axis=0)

    write_vec = lax.dynamic_index_in_dim(state_proj[:, 0], group, 1, keepdims=False)
    read_vec = lax.dynamic_index_in_dim(state_proj[:, 1], group, 1, keepdims=False)
    scores = lax.dot_general(
        read_vec, write_vec, (((1,), (1,)), ((), ())), preferred_element_type=jnp.float32
    )

    values = project_values(pieces, value_weights, tok, depth)
    values3 = values.reshape(tok, heads, HEAD_DIM)

    span_total = cum_rate[tok - 1]
    write_weighted = (
        jnp.exp(-(span_total[None] - cum_rate))[:, :, None]
        * write_vec[:, None, :].astype(jnp.float32)
    ).astype(jnp.bfloat16)
    ends = jnp.einsum(
        "thn,thp->hpn", write_weighted, values3, preferred_element_type=jnp.float32
    )

    mine = ends.astype(jnp.bfloat16)
    sibling = swap_ctx(mine, 1)
    my_total = lax.dynamic_index_in_dim(totals, me, 0, keepdims=False)
    sibling_total = lax.dynamic_index_in_dim(totals, me ^ 1, 0, keepdims=False)

    def fade(rate):
        return jnp.exp(-rate)

    own_scale = jnp.where(core == 0, fade(sibling_total), 1.0)
    sibling_scale = jnp.where(core == 0, 1.0, fade(my_total))
    plane_end = own_scale[:, None, None] * ends + sibling_scale[:, None, None] * sibling.astype(jnp.float32)
    share = heads // 2
    plane_share = lax.dynamic_slice_in_dim(plane_end, core * share, share, 0)
    plane_sent = plane_share.astype(jnp.bfloat16)
    near_sent = swap_ctx(plane_sent, 2)
    plane_totals = totals.reshape(CTX // 2, 2, heads).sum(axis=1)
    share_totals = lax.dynamic_slice_in_dim(plane_totals, core * share, share, 1)

    def joined(own, other, bit, at):
        group_totals = share_totals.reshape(-1, bit, share).sum(axis=1)
        later = lax.dynamic_index_in_dim(group_totals, at | 1, 0, keepdims=False)
        faded = fade(later)[:, None, None]
        own_is_later = (at & 1) == 1
        return jnp.where(own_is_later, own, other) + faded * jnp.where(own_is_later, other, own)

    pair = joined(plane_share, near_sent.astype(jnp.float32), 1, plane)
    pair_other = swap_ctx(pair.astype(jnp.bfloat16), 4)
    quad = joined(pair, pair_other.astype(jnp.float32), 2, plane // 2)
    quad_other = lax.ppermute(
        quad.astype(jnp.bfloat16),
        "ctx",
        [(2 * z + c, 2 * (7 - z) + c) for z in range(4) for c in range(2)],
    )
    shared = jnp.stack([near_sent, pair_other, quad_other])
    shared_other = swap_ctx(shared, 1)
    lower = jnp.where(core == 0, shared, shared_other)
    upper = jnp.where(core == 0, shared_other, shared)
    states = jnp.concatenate([sibling[None], jnp.concatenate([lower, upper], axis=1)], axis=0)

    level_fade = []
    for level in range(4):
        last = (me >> level << level) - 1
        there = (me >> level) & 1
        since = jnp.sum(
            jnp.where(((block > last) & (block < me))[:, None], totals, 0.0), axis=0
        )
        level_fade.append(jnp.where(there == 1, fade(since), 0.0))
    level_fade = jnp.stack(level_fade)

    prior_read = jnp.einsum(
        "tn,hpn->thp", read_vec.astype(jnp.float32), prior_state, precision=HIGH
    )
    cum_fade = jnp.exp(-cum_rate)
    rate_lag = cum_rate.T[:, :, None] - cum_rate.T[:, None, :]
    mixing = (
        jnp.where(causal[None], jnp.exp(-jnp.where(causal[None], rate_lag, 0.0)), 0.0) * scores[None]
    ).astype(jnp.bfloat16)
    local_out = jnp.einsum("hts,shp->thp", mixing, values3, preferred_element_type=jnp.float32)
    prior_scale = read_weights[5] * (cum_fade * fade(start_rate)[None])
    early = (
        read_weights[0][:, :, None] * local_out
        + prior_scale[:, :, None] * prior_read
        + skip_weight[None, :, None] * values3.astype(jnp.float32)
    )
    level_read = jnp.einsum(
        "tn,lhpn->lthp", read_vec, states, preferred_element_type=jnp.float32
    )
    level_scale = read_weights[1:5] * (cum_fade[None] * level_fade[:, None])
    mixed = early + jnp.sum(level_scale[:, :, :, None] * level_read, axis=0)

    return finish(
        pieces, gate_weights, mixed.reshape(tok, heads * HEAD_DIM), norm_gain[None]
    )


def solution(mesh):
    in_specs = (
        P("ctx", "tp"),
        P("ctx", "tp"),
        P("ctx", "tp"),
        P("ctx", None, None, None),
        P("ctx", "tp"),
        P(None, "ctx", "tp"),
        P("tp", None, None),
        P("tp"),
        P("tp"),
    )
    out_specs = P("ctx", "tp")
    return jax.shard_map(
        on_device, mesh=mesh, in_specs=in_specs, out_specs=out_specs, check_vma=False
    )
```

```python
import jax
import jax.numpy as jnp
from jax import lax
from jax.experimental import pallas as pl
from jax.experimental.pallas import tpu as pltpu
from jax.sharding import PartitionSpec as P

HEAD_DIM = 64
STATE = 256
HPG = 32
LEVELS = 6
HIGH = lax.Precision.HIGHEST
CTX = 16
SIDE = 4
HBM = pl.BlockSpec(memory_space=pltpu.HBM)
VMEM = pl.BlockSpec(memory_space=pltpu.VMEM)


def along_x(a, step):
    pairs = [(i, (i // SIDE) * SIDE + (i + step) % SIDE) for i in range(SIDE * SIDE)]
    return lax.ppermute(a, "tp", pairs)


def along_y(a, step):
    pairs = [(i, (i + SIDE * step) % (SIDE * SIDE)) for i in range(SIDE * SIDE)]
    return lax.ppermute(a, "tp", pairs)


def swap_ctx(a, mask):
    return lax.ppermute(a, "ctx", [(i, i ^ mask) for i in range(CTX)])


OFFSETS = (0, -1, 1, 2)
GROUPS = (1, 2, 4, 4, 3, 1, 1)


def in_hbm(*arrays):
    return [pltpu.with_memory_space_constraint(a, pltpu.HBM) for a in arrays]


def copies(moves, sem):
    started = []
    for i, (source, target) in enumerate(moves):
        copy = pltpu.make_async_copy(source, target, sem.at[i])
        copy.start()
        started.append(copy)
    for copy in started:
        copy.wait()


def stack_kernel(*refs):
    sources, targets = refs[:10], refs[10:12]
    held, in_sem, out_sem = refs[12:]
    moves = []
    for line in range(2):
        at = 0
        for source in sources[5 * line : 5 * line + 5]:
            rows = source.shape[0]
            moves.append((source, held.at[line, pl.ds(at, rows)]))
            at += rows
    copies(moves, in_sem)
    copies([(held.at[line], targets[line]) for line in range(2)], out_sem)


def stack(line_a, line_b):
    rows = sum(a.shape[0] for a in line_a)
    cols = line_a[0].shape[1]
    shape = jax.ShapeDtypeStruct((rows, cols), jnp.bfloat16)
    return pl.pallas_call(
        stack_kernel,
        out_shape=(shape, shape),
        in_specs=[HBM] * 10,
        out_specs=(HBM, HBM),
        scratch_shapes=[
            pltpu.VMEM((2, rows, cols), jnp.bfloat16),
            pltpu.SemaphoreType.DMA((10,)),
            pltpu.SemaphoreType.DMA((2,)),
        ],
    )(*in_hbm(*line_a, *line_b))


def gather_rows(rows):
    half = rows.shape[0] // 2
    top, bottom = rows[:half], rows[half:]
    near = along_x(top, 1), along_x(top, -1), along_y(bottom, 1), along_y(bottom, -1)
    cut = half // 2
    part = (near[0][:cut], near[1][cut:], near[2][:cut], near[3][cut:])
    far = along_x(part[0], 1), along_x(part[1], -1), along_y(part[2], 1), along_y(part[3], -1)
    line_a, line_b = stack((top, *near[:2], *far[:2]), (bottom, *near[2:], *far[2:]))
    next_ = along_y(line_a, 1), along_y(line_a, -1), along_x(line_b, 1), along_x(line_b, -1)
    part = (next_[0][: 2 * half], next_[1][2 * half :], next_[2][: 2 * half], next_[3][2 * half :])
    last = along_y(part[0], 1), along_y(part[1], -1), along_x(part[2], 1), along_x(part[3], -1)
    return (line_a, *next_[:2], *last[:2]), (line_b, *next_[2:], *last[2:])


def fetch_weights(w_ref, weights, sem, k, slot, depth):
    apart = w_ref.shape[0] // 16
    pltpu.make_async_copy(
        w_ref.at[pl.ds(pl.multiple_of(k * apart, 16), depth)],
        weights.at[pl.ds(slot * depth, depth)],
        sem.at[slot],
    ).start()


def sources_of_slots():
    tp = lax.axis_index("tp")
    y, x = tp // SIDE, tp % SIDE
    return [
        (i, j, ((y + dy + SIDE) % SIDE) * SIDE + (x + dx + SIDE) % SIDE)
        for j, dy in enumerate(OFFSETS)
        for i, dx in enumerate(OFFSETS)
    ]


def multiply(rows, weights, total, row_sem, weight_sem):
    deep = rows.shape[1]
    depth = deep // 16
    first = 0
    for group in GROUPS:
        for s in range(first, first + group):
            columns = pl.ds(s * depth, depth)
            pltpu.make_async_copy(rows.at[:, columns], rows.at[:, columns], row_sem.at[s]).wait()
            pltpu.make_async_copy(weights.at[columns], weights.at[columns], weight_sem.at[s]).wait()
        span = pl.ds(first * depth, group * depth)
        product = jnp.dot(rows[:, span], weights[span], preferred_element_type=jnp.float32)
        if first == 0:
            total[...] = product
        else:
            total[...] += product
        first += group


def project_cost(tok, cols, deep):
    return pl.CostEstimate(
        flops=2 * tok * cols * deep, bytes_accessed=2 * deep * (tok + cols), transcendentals=0
    )


def fetch_and_multiply(refs, w_ref, rows, weights, total, row_sem, weight_sem):
    pieces_a, pieces_b = refs[0:5], refs[5:10]
    tok, deep = rows.shape
    depth = deep // 16
    part = tok // 2

    def piece(pieces, near, far):
        if far < 3:
            return pieces[far].at[pl.ds(near * part, part)]
        return pieces[3 + near // 2].at[pl.ds((near % 2) * part, part)]

    for slot, (i, j, k) in enumerate(sources_of_slots()):
        columns = pl.ds(slot * depth, depth)
        pltpu.make_async_copy(
            piece(pieces_a, i, j), rows.at[pl.ds(0, part), columns], row_sem.at[slot]
        ).start()
        pltpu.make_async_copy(
            piece(pieces_b, j, i), rows.at[pl.ds(part, part), columns], row_sem.at[slot]
        ).start()
        fetch_weights(w_ref, weights, weight_sem, k, slot, depth)
    multiply(rows, weights, total, row_sem, weight_sem)


def project_scratch(tok, cols, deep):
    return [
        pltpu.VMEM((tok, deep), jnp.bfloat16),
        pltpu.VMEM((deep, cols), jnp.bfloat16),
        pltpu.VMEM((tok, cols), jnp.float32),
        pltpu.SemaphoreType.DMA((16,)),
        pltpu.SemaphoreType.DMA((16,)),
    ]


def values_kernel(*refs):
    values_out, total = refs[11], refs[14]
    fetch_and_multiply(refs[:10], refs[10], *refs[12:])
    values_out[...] = total[...].astype(values_out.dtype)


def project_values(pieces, w_full, tok, depth):
    cols = w_full.shape[1]
    deep = 16 * depth
    return pl.pallas_call(
        values_kernel,
        out_shape=jax.ShapeDtypeStruct((tok, cols), jnp.bfloat16),
        in_specs=[HBM] * 11,
        out_specs=VMEM,
        scratch_shapes=project_scratch(tok, cols, deep),
        compiler_params=pltpu.CompilerParams(vmem_limit_bytes=40 * 2**20),
        cost_estimate=project_cost(tok, cols, deep),
    )(*in_hbm(*pieces, w_full))


def gates_kernel(*refs):
    mixed_ref, gain_ref, out_ref = refs[11:14]
    total = refs[16]
    fetch_and_multiply(refs[:10], refs[10], *refs[14:])
    tok, cols = total.shape
    lanes = 128
    owner = lax.broadcasted_iota(jnp.int32, (cols, lanes), 0) // HEAD_DIM
    head = lax.broadcasted_iota(jnp.int32, (cols, lanes), 1)
    pick = jnp.where(owner == head, 1.0, 0.0).astype(jnp.bfloat16)
    gain = gain_ref[...]

    def select(a, axis):
        high = a.astype(jnp.bfloat16)
        low = (a - high.astype(jnp.float32)).astype(jnp.bfloat16)
        dims = (((1,), (axis,)), ((), ()))
        return lax.dot_general(high, pick, dims, preferred_element_type=jnp.float32) + lax.dot_general(
            low, pick, dims, preferred_element_type=jnp.float32
        )

    chunk = 64
    for first in range(0, tok, chunk):
        span = pl.ds(first, chunk)
        gates = total[span].astype(jnp.bfloat16).astype(jnp.float32)
        gated = mixed_ref[span] * (gates / (1.0 + jnp.exp(-gates)))
        inverse = lax.rsqrt(select(gated * gated, 0) * (1.0 / HEAD_DIM) + 1e-05)
        out_ref[span] = (gated * select(inverse, 1) * gain).astype(out_ref.dtype)


def finish(pieces, w_full, mixed, gain):
    deep, cols = w_full.shape
    tok = mixed.shape[0]
    return pl.pallas_call(
        gates_kernel,
        out_shape=jax.ShapeDtypeStruct((tok, cols), jnp.bfloat16),
        in_specs=[HBM] * 11 + [VMEM, VMEM],
        out_specs=VMEM,
        scratch_shapes=project_scratch(tok, cols, deep),
        compiler_params=pltpu.CompilerParams(vmem_limit_bytes=40 * 2**20),
        cost_estimate=project_cost(tok, cols, deep),
    )(*in_hbm(*pieces, w_full), mixed, gain)


def on_device(
    hidden_rows,
    w_value,
    w_gate,
    state_proj,
    rates,
    read_weights,
    prior_state,
    skip_weight,
    norm_gain,
):
    tok, heads = rates.shape
    me = lax.axis_index("ctx")
    core = me % 2
    plane = me // 2

    depth = hidden_rows.shape[1]

    rest = jnp.sum(rates, axis=0)
    terms = []
    for _ in range(3):
        terms.append(lax.reduce_precision(rest, 8, 7))
        rest = rest - terms[-1]
    tail = jnp.pad(jnp.stack(terms).astype(jnp.bfloat16), ((0, 13), (0, w_value.shape[1] - heads)))
    value_weights = lax.all_gather(
        jnp.concatenate([w_value, tail], axis=0), "ctx", axis=0, tiled=True
    )
    gate_weights = lax.all_gather(w_gate, "ctx", axis=0, tiled=True)
    pieces_a, pieces_b = gather_rows(hidden_rows)
    group = lax.axis_index("tp") * heads // HPG
    rates, prior_state, read_weights, group, line = lax.optimization_barrier(
        (rates, prior_state, read_weights, group, pieces_a[0])
    )
    pieces = (line, *pieces_a[1:], *pieces_b)

    order = jnp.arange(tok)
    causal = order[:, None] >= order[None, :]
    cum_rate = jnp.dot(causal.astype(jnp.float32), rates, precision=HIGH)
    totals = value_weights.reshape(CTX, depth + 16, -1)[:, depth : depth + 3, :heads]
    totals = jnp.sum(totals.astype(jnp.float32), axis=1)
    block = jnp.arange(CTX, dtype=jnp.int32)
    start_rate = jnp.sum(jnp.where((block < me)[:, None], totals, 0.0), axis=0)

    write_vec = lax.dynamic_index_in_dim(state_proj[:, 0], group, 1, keepdims=False)
    read_vec = lax.dynamic_index_in_dim(state_proj[:, 1], group, 1, keepdims=False)
    scores = lax.dot_general(
        read_vec, write_vec, (((1,), (1,)), ((), ())), preferred_element_type=jnp.float32
    )

    values = project_values(pieces, value_weights, tok, depth)
    values3 = values.reshape(tok, heads, HEAD_DIM)

    span_total = cum_rate[tok - 1]
    write_weighted = (
        jnp.exp(-(span_total[None] - cum_rate))[:, :, None]
        * write_vec[:, None, :].astype(jnp.float32)
    ).astype(jnp.bfloat16)
    ends = jnp.einsum(
        "thn,thp->hpn", write_weighted, values3, preferred_element_type=jnp.float32
    )

    mine = ends.astype(jnp.bfloat16)
    sibling = swap_ctx(mine, 1)
    my_total = lax.dynamic_index_in_dim(totals, me, 0, keepdims=False)
    sibling_total = lax.dynamic_index_in_dim(totals, me ^ 1, 0, keepdims=False)

    def fade(rate):
        return jnp.exp(-rate)

    own_scale = jnp.where(core == 0, fade(sibling_total), 1.0)
    sibling_scale = jnp.where(core == 0, 1.0, fade(my_total))
    plane_end = own_scale[:, None, None] * ends + sibling_scale[:, None, None] * sibling.astype(jnp.float32)
    share = heads // 2
    plane_share = lax.dynamic_slice_in_dim(plane_end, core * share, share, 0)
    plane_sent = plane_share.astype(jnp.bfloat16)
    near_sent = swap_ctx(plane_sent, 2)
    values_late, _ = lax.optimization_barrier((values3, plane_sent))
    prior_read = jnp.einsum(
        "tn,hpn->thp", read_vec.astype(jnp.float32), prior_state, precision=HIGH
    )
    cum_fade = jnp.exp(-cum_rate)
    rate_lag = cum_rate.T[:, :, None] - cum_rate.T[:, None, :]
    mixing = (
        jnp.where(causal[None], jnp.exp(-jnp.where(causal[None], rate_lag, 0.0)), 0.0) * scores[None]
    ).astype(jnp.bfloat16)
    local_out = jnp.einsum("hts,shp->thp", mixing, values_late, preferred_element_type=jnp.float32)
    prior_scale = read_weights[5] * (cum_fade * fade(start_rate)[None])
    early = (
        read_weights[0][:, :, None] * local_out
        + prior_scale[:, :, None] * prior_read
        + skip_weight[None, :, None] * values3.astype(jnp.float32)
    )
    plane_totals = totals.reshape(CTX // 2, 2, heads).sum(axis=1)
    share_totals = lax.dynamic_slice_in_dim(plane_totals, core * share, share, 1)

    def joined(own, other, bit, at):
        group_totals = share_totals.reshape(-1, bit, share).sum(axis=1)
        later = lax.dynamic_index_in_dim(group_totals, at | 1, 0, keepdims=False)
        faded = fade(later)[:, None, None]
        own_is_later = (at & 1) == 1
        return jnp.where(own_is_later, own, other) + faded * jnp.where(own_is_later, other, own)

    pair = joined(plane_share, near_sent.astype(jnp.float32), 1, plane)
    pair_sent, early = lax.optimization_barrier((pair.astype(jnp.bfloat16), early))
    pair_other = swap_ctx(pair_sent, 4)
    quad = joined(pair, pair_other.astype(jnp.float32), 2, plane // 2)
    quad_other = lax.ppermute(
        quad.astype(jnp.bfloat16),
        "ctx",
        [(2 * z + c, 2 * (7 - z) + c) for z in range(4) for c in range(2)],
    )
    shared = jnp.stack([near_sent, pair_other, quad_other])
    shared_other = swap_ctx(shared, 1)
    lower = jnp.where(core == 0, shared, shared_other)
    upper = jnp.where(core == 0, shared_other, shared)
    states = jnp.concatenate([sibling[None], jnp.concatenate([lower, upper], axis=1)], axis=0)

    level_fade = []
    for level in range(4):
        last = (me >> level << level) - 1
        there = (me >> level) & 1
        since = jnp.sum(
            jnp.where(((block > last) & (block < me))[:, None], totals, 0.0), axis=0
        )
        level_fade.append(jnp.where(there == 1, fade(since), 0.0))
    level_fade = jnp.stack(level_fade)

    level_read = jnp.einsum(
        "tn,lhpn->lthp", read_vec, states, preferred_element_type=jnp.float32
    )
    level_scale = read_weights[1:5] * (cum_fade[None] * level_fade[:, None])
    mixed = early + jnp.sum(level_scale[:, :, :, None] * level_read, axis=0)

    return finish(
        pieces, gate_weights, mixed.reshape(tok, heads * HEAD_DIM), norm_gain[None]
    )


def solution(mesh):
    in_specs = (
        P("ctx", "tp"),
        P("ctx", "tp"),
        P("ctx", "tp"),
        P("ctx", None, None, None),
        P("ctx", "tp"),
        P(None, "ctx", "tp"),
        P("tp", None, None),
        P("tp"),
        P("tp"),
    )
    out_specs = P("ctx", "tp")
    return jax.shard_map(
        on_device, mesh=mesh, in_specs=in_specs, out_specs=out_specs, check_vma=False
    )
```
